32 devices in a mesh: ctx: 8 (over y, x, core), section: 4 (over z).
Axes of the slice: x: 2, y: 2, z: 4, core: 2. Of those that a mesh axis runs over, the one named last changes fastest.
Arguments:
- query_in: bfloat16 [4, 4, 8192], P('section', None, 'ctx'), may hold values from -100 to 100
- keys: bfloat16 [4, 4, 8192, 4, 128], P('section', None, 'ctx'), may hold values from -6 to 6
- values: bfloat16 [4, 4, 8192, 4, 128], P('section', None, 'ctx'), may hold values from -6 to 6
- lengths: int32 [4, 8], P(None, 'ctx'), may hold values from 256 to 1024, as said below
Outputs:
- attended: bfloat16 [4, 4, 8192], P('section', None, 'ctx')
The draws below stay inside these ranges and needn't reach their ends.
Inputs may be any that keep to these rules, and one draw needn't show every extreme that they name: `lengths`: each request has one slab with all 1024 positions live.
All inputs are finite; a program needn't handle non-finite values.
Results may differ from the reference program's by a relative error of at most 0.028.
Values may be sent and summed in bfloat16 or wider, within the bound.
A program may use at most 64 MiB of HBM per device.

```python
import math
import jax
import jax.numpy as jnp
from jax import lax

QH = 64
KVH = 4
HD = 128
REQ = 4
TOK_DEV = 1024
LAYERS = 4
SLABS = 8
TOKENS = 8192


def shared_parts(key):
    subkeys = jax.random.split(jax.random.fold_in(key, 7), 6)
    sign_table = jnp.where(jax.random.bernoulli(subkeys[0], 0.5, (REQ, KVH, HD)), 1.0, -1.0).astype(jnp.float32)
    first_offset = jax.random.randint(subkeys[5], (REQ, SLABS), 0, TOK_DEV // 4 - 1)
    positions = jnp.arange(TOKENS, dtype=jnp.int32)
    slab_start = first_offset[:, positions // TOK_DEV]
    from_start = (positions % TOK_DEV)[None, :] - slab_start
    return (sign_table, from_start)


def draw_keys(key, part):
    sign_table, from_start = shared_parts(key)
    key = jax.random.fold_in(key, 11)
    full_shape = (LAYERS, REQ, TOKENS, KVH, HD)
    sample = jnp.clip(jax.random.normal(key, full_shape, jnp.float32), -6.0, 6.0)
    narrowed = jnp.ones((LAYERS, REQ, 1, KVH, 1), jnp.float32)
    offset_mark = from_start[None, :, :, None, None]
    direction = sign_table[None, :, None, :, :]
    planted_scale = jnp.where(offset_mark == 0, 3.0, 3.0 * narrowed)
    planted = planted_scale * direction + 0.05 * sample
    chosen = jnp.where((offset_mark == 0) | (offset_mark == 1), planted, sample)
    return chosen.astype(jnp.bfloat16)


def draw_values(key, part):
    sign_table, from_start = shared_parts(key)
    key = jax.random.fold_in(key, 19)
    full_shape = (LAYERS, REQ, TOKENS, KVH, HD)
    sample = jnp.clip(jax.random.normal(key, full_shape, jnp.float32), -5.0, 5.0)
    offset_mark = from_start[None, :, :, None, None]
    common_part = jnp.where((offset_mark == 0) | (offset_mark == 1), -0.75, 0.75)
    chosen = common_part * sign_table[None, :, None, :, :] + sample
    return chosen.astype(jnp.bfloat16)


def draw_query_in(key, part):
    key = jax.random.fold_in(key, 13)
    noise_key = jax.random.fold_in(key, 0)
    sample = jnp.clip(jax.random.normal(noise_key, (LAYERS, REQ, QH * HD), jnp.float32), -6.0, 6.0)
    return sample.astype(jnp.bfloat16)


def draw_lengths(key, part):
    key = jax.random.fold_in(key, 17)
    span_key, full_key = jax.random.split(key)
    span_draw = jax.random.randint(span_key, (REQ, SLABS), TOK_DEV // 4, TOK_DEV + 1)
    full_slab = jax.random.randint(full_key, (REQ, 1), 0, SLABS)
    slab_ids = jnp.arange(SLABS, dtype=jnp.int32)[None, :]
    return jnp.where(slab_ids == full_slab, TOK_DEV, span_draw).astype(jnp.int32)


def setup_inputs(seed: int = 0) -> dict:
    arg_keys = jax.random.split(jax.random.key(seed), 5)
    query_in = draw_query_in(jax.random.fold_in(arg_keys[4], 71), 0)
    keys = draw_keys(jax.random.fold_in(arg_keys[4], 71), 0)
    values = draw_values(jax.random.fold_in(arg_keys[4], 71), 0)
    lengths = draw_lengths(jax.random.fold_in(arg_keys[4], 71), 0)
    return dict(query_in=query_in, keys=keys, values=values, lengths=lengths)


def reference(query_in, keys, values, lengths):
    group_size = QH // KVH
    score_scale = 1.0 / math.sqrt(HD)
    positions = jnp.arange(TOKENS, dtype=jnp.int32)
    slab_of = positions // TOK_DEV
    live_mask = (positions % TOK_DEV)[None, :] < lengths[:, slab_of]
    residual = jnp.zeros((REQ, QH * HD), jnp.float32)
    layer_outputs = []
    for layer_no in range(LAYERS):
        query_rows = (query_in[layer_no].astype(jnp.float32) + residual).astype(jnp.bfloat16)
        grouped = query_rows.reshape(REQ, KVH, group_size, HD).astype(jnp.float32)
        key_rows = keys[layer_no].astype(jnp.float32)
        scores = jnp.einsum('rgqd,rtgd->rgqt', grouped, key_rows) * score_scale
        scores = jnp.where(live_mask[:, None, None, :], scores, -jnp.inf)
        row_peak = lax.optimization_barrier(jnp.max(scores, axis=-1, keepdims=True))
        weights = jnp.exp(scores - row_peak)
        row_total = lax.optimization_barrier(jnp.sum(weights, axis=-1))
        rounded = weights.astype(jnp.bfloat16).astype(jnp.float32)
        summed = jnp.einsum('rgqt,rtgd->rgqd', rounded, values[layer_no].astype(jnp.float32))
        mixed = (summed / row_total[..., None]).reshape(REQ, QH * HD)
        layer_outputs.append(mixed.astype(jnp.bfloat16))
        residual = residual + mixed
    return jnp.stack(layer_outputs)
```

```python
import functools
import math

import jax
import jax.numpy as jnp
from jax import lax
from jax.experimental import pallas as pl
from jax.experimental.pallas import tpu as pltpu
from jax.sharding import PartitionSpec as P

MESH = pl.DeviceIdType.MESH
DEAD = -1e30
CHUNK = 512


def wait_bytes(ref, sem):
    pltpu.make_async_copy(ref, ref, sem).wait()


def kernel(
    dims, lengths, query, keys, values, out,
    key_buf, value_buf, bias, query_all, residual, state_out, state_in, hand_on, result,
    key_sem, value_sem, query_send, query_recv, state_send, state_recv, hand_send, hand_recv,
):
    slabs, sections, requests, own, kv_heads, span, head_dim, rows = dims
    ctx = lax.axis_index("ctx")
    section = lax.axis_index("section")
    heads = own * slabs
    group = heads // kv_heads
    width = span * kv_heads
    factor = math.log2(math.e) / math.sqrt(head_dim)
    has_next = section < sections - 1
    has_previous = section > 0
    before = jnp.maximum(section - 1, 0)
    after = jnp.minimum(section + 1, sections - 1)

    def load(r):
        return (
            pltpu.make_async_copy(keys.at[r], key_buf.at[r], key_sem.at[r]),
            pltpu.make_async_copy(values.at[r], value_buf.at[r], value_sem.at[r]),
        )

    barrier = pltpu.get_barrier_semaphore()
    for d in range(1, slabs):
        peer = lax.rem(ctx + d, slabs)
        pl.semaphore_signal(barrier, inc=1, device_id=(peer, section), device_id_type=MESH)

    @pl.when(has_previous)
    def _():
        for i in range(slabs):
            pl.semaphore_signal(barrier, inc=1, device_id=(i, before), device_id_type=MESH)

    for r in range(requests):
        for copy in load(r):
            copy.start()

    wide = query[...].astype(jnp.float32)
    for r in range(requests):
        for h in range(own):
            query_all[ctx, r, h : h + 1, :] = wide[r : r + 1, h * head_dim : (h + 1) * head_dim]

    pl.semaphore_wait(barrier, slabs - 1 + slabs * has_next.astype(jnp.int32))

    for d in range(1, slabs):
        peer = lax.rem(ctx + d, slabs)
        pltpu.make_async_remote_copy(
            src_ref=query_all.at[ctx], dst_ref=query_all.at[ctx],
            send_sem=query_send, recv_sem=query_recv,
            device_id=(peer, section), device_id_type=MESH,
        ).start()

    column = lax.broadcasted_iota(jnp.int32, (8, width), 1)
    for r in range(requests):
        alive = column < lengths[r] * kv_heads
        for g in range(kv_heads):
            bias[r, g] = jnp.where(alive & (lax.rem(column, kv_heads) == g), 0.0, DEAD)

    @pl.when(jnp.logical_not(has_previous))
    def _():
        residual[...] = jnp.zeros_like(residual)

    wait_bytes(query_all.at[pl.ds(0, slabs - 1)], query_recv)

    def attend(r):
        @pl.when(has_previous)
        def _():
            wait_bytes(residual.at[r], hand_recv.at[r])

        both = query_all[:, r] + residual[r]
        q = both[:, :own].reshape(heads, head_dim).astype(jnp.bfloat16)
        key_copy, value_copy = load(r)
        key_copy.wait()
        scores = []
        top = None
        for j in range(0, width, CHUNK):
            s = lax.dot_general(
                q, key_buf[r, j : j + CHUNK], (((1,), (1,)), ((), ())),
                preferred_element_type=jnp.float32,
            ) * factor
            s = s.reshape(kv_heads, group // 8, 8, CHUNK) + bias[r, :, :, j : j + CHUNK][:, None]
            s = s.reshape(heads, CHUNK)
            scores.append(s)
            top = s if top is None else jnp.maximum(top, s)
        peak = jnp.max(top, axis=-1, keepdims=True)
        value_copy.wait()
        mass = None
        mixed = None
        for n, j in enumerate(range(0, width, CHUNK)):
            w = jnp.exp2(scores[n] - peak)
            mass = w if mass is None else mass + w
            part = jnp.dot(
                w.astype(jnp.bfloat16), value_buf[r, j : j + CHUNK],
                preferred_element_type=jnp.float32,
            )
            mixed = part if mixed is None else mixed + part
        total = jnp.sum(mass, axis=-1, keepdims=True)
        mixed = mixed / total
        level = jnp.broadcast_to(peak + jnp.log2(total), (heads, head_dim))
        for i in range(slabs):
            state_out[r, i, 0, :own] = mixed[i * own : (i + 1) * own]
            state_out[r, i, 1, :own] = level[i * own : (i + 1) * own]
        for d in range(1, slabs):
            peer = lax.rem(ctx + d, slabs)
            pltpu.make_async_remote_copy(
                src_ref=state_out.at[r, peer], dst_ref=state_in.at[r, d - 1],
                send_sem=state_send.at[r], recv_sem=state_recv.at[r],
                device_id=(peer, section), device_id_type=MESH,
            ).start()

    def combine(r):
        wait_bytes(state_in.at[r], state_recv.at[r])
        parts = [state_out[r, ctx, 0, :own]] + [state_in[r, d, 0, :own] for d in range(slabs - 1)]
        levels = [state_out[r, ctx, 1, :own]] + [state_in[r, d, 1, :own] for d in range(slabs - 1)]
        top = functools.reduce(jnp.maximum, levels)
        shares = [jnp.exp2(level - top) for level in levels]
        mixed = sum(p * w for p, w in zip(parts, shares)) / sum(shares)

        @pl.when(has_next)
        def _():
            hand_on[r, :own] = residual[r, ctx, :own] + mixed
            for i in range(slabs):
                pltpu.make_async_remote_copy(
                    src_ref=hand_on.at[r], dst_ref=residual.at[r, ctx],
                    send_sem=hand_send.at[r], recv_sem=hand_recv.at[r],
                    device_id=(i, after), device_id_type=MESH,
                ).start()

        result[r, :own] = mixed

    def turn(r, _):
        @pl.when(r < requests)
        def _():
            attend(jnp.minimum(r, requests - 1))

        @pl.when(r > 0)
        def _():
            combine(jnp.maximum(r - 1, 0))

        return 0

    lax.fori_loop(0, requests + 1, turn, 0)

    for r in range(requests):
        for h in range(own):
            out[r : r + 1, h * head_dim : (h + 1) * head_dim] = result[r, h : h + 1, :]

    wait_bytes(query_all.at[pl.ds(0, slabs - 1)], query_send)
    for r in range(requests):
        wait_bytes(state_in.at[r], state_send.at[r])

    @pl.when(has_next)
    def _():
        for r in range(requests):
            wait_bytes(residual.at[r], hand_send.at[r])


def body(query_in, keys, values, lengths):
    sections = lax.axis_size("section")
    slabs = lax.axis_size("ctx")
    _, requests, span, kv_heads, head_dim = keys.shape
    own = query_in.shape[2] // head_dim
    rows = -(-own // 8) * 8
    width = span * kv_heads
    dims = (slabs, sections, requests, own, kv_heads, span, head_dim, rows)
    flat_keys = keys.reshape(requests, width, head_dim)
    flat_values = values.reshape(requests, width, head_dim)
    dma = pltpu.SemaphoreType.DMA
    f32 = jnp.float32
    result = pl.pallas_call(
        functools.partial(kernel, dims),
        out_shape=jax.ShapeDtypeStruct((requests, own * head_dim), f32),
        in_specs=[
            pl.BlockSpec(memory_space=pltpu.SMEM),
            pl.BlockSpec(memory_space=pltpu.VMEM),
            pl.BlockSpec(memory_space=pltpu.HBM),
            pl.BlockSpec(memory_space=pltpu.HBM),
        ],
        out_specs=pl.BlockSpec(memory_space=pltpu.VMEM),
        scratch_shapes=[
            pltpu.VMEM((requests, width, head_dim), jnp.bfloat16),
            pltpu.VMEM((requests, width, head_dim), jnp.bfloat16),
            pltpu.VMEM((requests, kv_heads, 8, width), f32),
            pltpu.VMEM((slabs, requests, rows, head_dim), f32),
            pltpu.VMEM((requests, slabs, rows, head_dim), f32),
            pltpu.VMEM((requests, slabs, 2, rows, head_dim), f32),
            pltpu.VMEM((requests, slabs - 1, 2, rows, head_dim), f32),
            pltpu.VMEM((requests, rows, head_dim), f32),
            pltpu.VMEM((requests, rows, head_dim), f32),
            dma((requests,)),
            dma((requests,)),
            dma,
            dma,
            dma((requests,)),
            dma((requests,)),
            dma((requests,)),
            dma((requests,)),
        ],
        compiler_params=pltpu.CompilerParams(
            collective_id=0, has_side_effects=True, vmem_limit_bytes=60 * 1024 * 1024
        ),
        name="layered_decode",
    )(lengths[:, 0], query_in[0], flat_keys, flat_values)
    return result.astype(jnp.bfloat16)[None]


def solution(mesh):
    return jax.shard_map(
        body,
        mesh=mesh,
        in_specs=(
            P("section", None, "ctx"),
            P("section", None, "ctx", None, None),
            P("section", None, "ctx", None, None),
            P(None, "ctx"),
        ),
        out_specs=P("section", None, "ctx"),
        check_vma=False,
    )
```

```python
import functools
import math

import jax
import jax.numpy as jnp
from jax import lax
from jax.experimental import pallas as pl
from jax.experimental.pallas import tpu as pltpu
from jax.sharding import PartitionSpec as P

MESH = pl.DeviceIdType.MESH
DEAD = -1e30
CHUNK = 512


def wait_bytes(ref, sem):
    pltpu.make_async_copy(ref, ref, sem).wait()


def kernel(
    dims, lengths_in, query_in, keys, values, out, lengths, query,
    key_buf, value_buf, bias, query_all, residual, state_out, state_in, hand_on, result,
    key_sem, value_sem, query_send, query_recv, state_send, state_recv, hand_send, hand_recv, small_sem,
):
    slabs, sections, requests, own, kv_heads, span, head_dim, rows = dims
    ctx = lax.axis_index("ctx")
    section = lax.axis_index("section")
    heads = own * slabs
    group = heads // kv_heads
    width = span * kv_heads
    factor = math.log2(math.e) / math.sqrt(head_dim)
    has_next = section < sections - 1
    has_previous = section > 0
    before = jnp.maximum(section - 1, 0)
    after = jnp.minimum(section + 1, sections - 1)

    def load(r):
        return (
            pltpu.make_async_copy(keys.at[r], key_buf.at[r], key_sem.at[r]),
            pltpu.make_async_copy(values.at[r], value_buf.at[r], value_sem.at[r]),
        )

    barrier = pltpu.get_barrier_semaphore()
    for d in range(1, slabs):
        peer = lax.rem(ctx + d, slabs)
        pl.semaphore_signal(barrier, inc=1, device_id=(peer, section), device_id_type=MESH)

    @pl.when(has_previous)
    def _():
        for i in range(slabs):
            pl.semaphore_signal(barrier, inc=1, device_id=(i, before), device_id_type=MESH)

    query_copy = pltpu.make_async_copy(query_in, query, small_sem.at[0])
    lengths_copy = pltpu.make_async_copy(lengths_in, lengths, small_sem.at[1])
    query_copy.start()
    lengths_copy.start()
    for r in range(requests):
        for copy in load(r):
            copy.start()
    query_copy.wait()

    wide = query[...].astype(jnp.float32)
    for r in range(requests):
        for h in range(own):
            query_all[ctx, r, h : h + 1, :] = wide[r : r + 1, h * head_dim : (h + 1) * head_dim]

    pl.semaphore_wait(barrier, slabs - 1 + slabs * has_next.astype(jnp.int32))

    for d in range(1, slabs):
        peer = lax.rem(ctx + d, slabs)
        pltpu.make_async_remote_copy(
            src_ref=query_all.at[ctx], dst_ref=query_all.at[ctx],
            send_sem=query_send, recv_sem=query_recv,
            device_id=(peer, section), device_id_type=MESH,
        ).start()

    lengths_copy.wait()
    column = lax.broadcasted_iota(jnp.int32, (8, width), 1)
    for r in range(requests):
        alive = column < lengths[r] * kv_heads
        for g in range(kv_heads):
            bias[r, g] = jnp.where(alive & (lax.rem(column, kv_heads) == g), 0.0, DEAD)

    @pl.when(jnp.logical_not(has_previous))
    def _():
        residual[...] = jnp.zeros_like(residual)

    wait_bytes(query_all.at[pl.ds(0, slabs - 1)], query_recv)

    def attend(r):
        @pl.when(has_previous)
        def _():
            wait_bytes(residual.at[r], hand_recv.at[r])

        both = query_all[:, r] + residual[r]
        q = both[:, :own].reshape(heads, head_dim).astype(jnp.bfloat16)
        key_copy, value_copy = load(r)
        key_copy.wait()
        scores = []
        top = None
        for j in range(0, width, CHUNK):
            s = lax.dot_general(
                q, key_buf[r, j : j + CHUNK], (((1,), (1,)), ((), ())),
                preferred_element_type=jnp.float32,
            ) * factor
            s = s.reshape(kv_heads, group // 8, 8, CHUNK) + bias[r, :, :, j : j + CHUNK][:, None]
            s = s.reshape(heads, CHUNK)
            scores.append(s)
            top = s if top is None else jnp.maximum(top, s)
        peak = jnp.max(top, axis=-1, keepdims=True)
        value_copy.wait()
        mass = None
        mixed = None
        for n, j in enumerate(range(0, width, CHUNK)):
            w = jnp.exp2(scores[n] - peak)
            mass = w if mass is None else mass + w
            part = jnp.dot(
                w.astype(jnp.bfloat16), value_buf[r, j : j + CHUNK],
                preferred_element_type=jnp.float32,
            )
            mixed = part if mixed is None else mixed + part
        total = jnp.sum(mass, axis=-1, keepdims=True)
        mixed = mixed / total
        level = jnp.broadcast_to(peak + jnp.log2(total), (heads, head_dim))
        for i in range(slabs):
            state_out[r, i, 0, :own] = mixed[i * own : (i + 1) * own]
            state_out[r, i, 1, :own] = level[i * own : (i + 1) * own]
        for d in range(1, slabs):
            peer = lax.rem(ctx + d, slabs)
            pltpu.make_async_remote_copy(
                src_ref=state_out.at[r, peer], dst_ref=state_in.at[r, d - 1],
                send_sem=state_send.at[r], recv_sem=state_recv.at[r],
                device_id=(peer, section), device_id_type=MESH,
            ).start()

    def combine(r):
        wait_bytes(state_in.at[r], state_recv.at[r])
        parts = [state_out[r, ctx, 0, :own]] + [state_in[r, d, 0, :own] for d in range(slabs - 1)]
        levels = [state_out[r, ctx, 1, :own]] + [state_in[r, d, 1, :own] for d in range(slabs - 1)]
        top = functools.reduce(jnp.maximum, levels)
        shares = [jnp.exp2(level - top) for level in levels]
        mixed = sum(p * w for p, w in zip(parts, shares)) / sum(shares)

        @pl.when(has_next)
        def _():
            hand_on[r, :own] = residual[r, ctx, :own] + mixed
            for i in range(slabs):
                pltpu.make_async_remote_copy(
                    src_ref=hand_on.at[r], dst_ref=residual.at[r, ctx],
                    send_sem=hand_send.at[r], recv_sem=hand_recv.at[r],
                    device_id=(i, after), device_id_type=MESH,
                ).start()

        result[r, :own] = mixed

    def attend_turn(r, _):
        attend(r)
        return 0

    def combine_turn(r, _):
        combine(r)
        return 0

    lax.fori_loop(0, requests, attend_turn, 0)
    lax.fori_loop(0, requests, combine_turn, 0)

    for r in range(requests):
        for h in range(own):
            out[r : r + 1, h * head_dim : (h + 1) * head_dim] = result[r, h : h + 1, :]

    wait_bytes(query_all.at[pl.ds(0, slabs - 1)], query_send)
    for r in range(requests):
        wait_bytes(state_in.at[r], state_send.at[r])

    @pl.when(has_next)
    def _():
        for r in range(requests):
            wait_bytes(residual.at[r], hand_send.at[r])


def body(query_in, keys, values, lengths):
    sections = lax.axis_size("section")
    slabs = lax.axis_size("ctx")
    _, requests, span, kv_heads, head_dim = keys.shape
    own = query_in.shape[2] // head_dim
    rows = -(-own // 8) * 8
    width = span * kv_heads
    dims = (slabs, sections, requests, own, kv_heads, span, head_dim, rows)
    flat_keys = keys.reshape(requests, width, head_dim)
    flat_values = values.reshape(requests, width, head_dim)
    dma = pltpu.SemaphoreType.DMA
    f32 = jnp.float32
    result = pl.pallas_call(
        functools.partial(kernel, dims),
        out_shape=jax.ShapeDtypeStruct((requests, own * head_dim), f32),
        in_specs=[
            pl.BlockSpec(memory_space=pltpu.HBM),
            pl.BlockSpec(memory_space=pltpu.HBM),
            pl.BlockSpec(memory_space=pltpu.HBM),
            pl.BlockSpec(memory_space=pltpu.HBM),
        ],
        out_specs=pl.BlockSpec(memory_space=pltpu.VMEM),
        scratch_shapes=[
            pltpu.SMEM((requests,), jnp.int32),
            pltpu.VMEM((requests, own * head_dim), jnp.bfloat16),
            pltpu.VMEM((requests, width, head_dim), jnp.bfloat16),
            pltpu.VMEM((requests, width, head_dim), jnp.bfloat16),
            pltpu.VMEM((requests, kv_heads, 8, width), f32),
            pltpu.VMEM((slabs, requests, rows, head_dim), f32),
            pltpu.VMEM((requests, slabs, rows, head_dim), f32),
            pltpu.VMEM((requests, slabs, 2, rows, head_dim), f32),
            pltpu.VMEM((requests, slabs - 1, 2, rows, head_dim), f32),
            pltpu.VMEM((requests, rows, head_dim), f32),
            pltpu.VMEM((requests, rows, head_dim), f32),
            dma((requests,)),
            dma((requests,)),
            dma,
            dma,
            dma((requests,)),
            dma((requests,)),
            dma((requests,)),
            dma((requests,)),
            dma((2,)),
        ],
        compiler_params=pltpu.CompilerParams(
            collective_id=0, has_side_effects=True, vmem_limit_bytes=60 * 1024 * 1024
        ),
        name="layered_decode",
    )(lengths[:, 0], query_in[0], flat_keys, flat_values)
    return result.astype(jnp.bfloat16)[None]


def solution(mesh):
    return jax.shard_map(
        body,
        mesh=mesh,
        in_specs=(
            P("section", None, "ctx"),
            P("section", None, "ctx", None, None),
            P("section", None, "ctx", None, None),
            P(None, "ctx"),
        ),
        out_specs=P("section", None, "ctx"),
        check_vma=False,
    )
```

```python
import functools
import math

import jax
import jax.numpy as jnp
from jax import lax
from jax.experimental import pallas as pl
from jax.experimental.pallas import tpu as pltpu
from jax.sharding import PartitionSpec as P

MESH = pl.DeviceIdType.MESH
DEAD = -1e30
CHUNK = 512


def wait_bytes(ref, sem):
    pltpu.make_async_copy(ref, ref, sem).wait()


def kernel(
    dims, lengths_in, query_in, keys, values, out, lengths, query,
    key_buf, value_buf, bias, query_all, residual, state_out, state_in, hand_on, result,
    key_sem, value_sem, query_send, query_recv, state_send, state_recv, hand_send, hand_recv, small_sem,
):
    slabs, sections, requests, own, kv_heads, span, head_dim, rows = dims
    ctx = lax.axis_index("ctx")
    section = lax.axis_index("section")
    heads = own * slabs
    group = heads // kv_heads
    width = span * kv_heads
    factor = math.log2(math.e) / math.sqrt(head_dim)
    has_next = section < sections - 1
    has_previous = section > 0
    before = jnp.maximum(section - 1, 0)
    after = jnp.minimum(section + 1, sections - 1)

    def load(r):
        return (
            pltpu.make_async_copy(keys.at[r], key_buf.at[r], key_sem.at[r]),
            pltpu.make_async_copy(values.at[r], value_buf.at[r], value_sem.at[r]),
        )

    barrier = pltpu.get_barrier_semaphore()
    for d in range(1, slabs):
        peer = lax.rem(ctx + d, slabs)
        pl.semaphore_signal(barrier, inc=1, device_id=(peer, section), device_id_type=MESH)

    @pl.when(has_previous)
    def _():
        for i in range(slabs):
            pl.semaphore_signal(barrier, inc=1, device_id=(i, before), device_id_type=MESH)

    query_copy = pltpu.make_async_copy(query_in, query, small_sem.at[0])
    lengths_copy = pltpu.make_async_copy(lengths_in, lengths, small_sem.at[1])
    query_copy.start()
    lengths_copy.start()
    for r in range(requests):
        for copy in load(r):
            copy.start()
    query_copy.wait()

    wide = query[...].astype(jnp.float32)
    for r in range(requests):
        for h in range(own):
            query_all[ctx, r, h : h + 1, :] = wide[r : r + 1, h * head_dim : (h + 1) * head_dim]

    pl.semaphore_wait(barrier, slabs - 1 + slabs * has_next.astype(jnp.int32))

    firsts = pl.ds(0, 1)
    others = pl.ds(1, requests - 1)
    arrivals = pl.ds(0, slabs - 1)
    for part, span_of in enumerate((firsts, others)):
        for d in range(1, slabs):
            peer = lax.rem(ctx + d, slabs)
            pltpu.make_async_remote_copy(
                src_ref=query_all.at[ctx, span_of], dst_ref=query_all.at[ctx, span_of],
                send_sem=query_send.at[part], recv_sem=query_recv.at[part],
                device_id=(peer, section), device_id_type=MESH,
            ).start()

    lengths_copy.wait()
    column = lax.broadcasted_iota(jnp.int32, (8, width), 1)
    for r in range(requests):
        alive = column < lengths[r] * kv_heads
        for g in range(kv_heads):
            bias[r, g] = jnp.where(alive & (lax.rem(column, kv_heads) == g), 0.0, DEAD)

    @pl.when(jnp.logical_not(has_previous))
    def _():
        residual[...] = jnp.zeros_like(residual)

    wait_bytes(query_all.at[arrivals, firsts], query_recv.at[0])

    def attend(r):
        @pl.when(r == 1)
        def _():
            wait_bytes(query_all.at[arrivals, others], query_recv.at[1])

        @pl.when(has_previous)
        def _():
            wait_bytes(residual.at[r], hand_recv.at[r])

        both = query_all[:, r] + residual[r]
        q = both[:, :own].reshape(heads, head_dim).astype(jnp.bfloat16)
        key_copy, value_copy = load(r)
        key_copy.wait()
        scores = []
        top = None
        for j in range(0, width, CHUNK):
            s = lax.dot_general(
                q, key_buf[r, j : j + CHUNK], (((1,), (1,)), ((), ())),
                preferred_element_type=jnp.float32,
            ) * factor
            s = s.reshape(kv_heads, group // 8, 8, CHUNK) + bias[r, :, :, j : j + CHUNK][:, None]
            s = s.reshape(heads, CHUNK)
            scores.append(s)
            top = s if top is None else jnp.maximum(top, s)
        peak = jnp.max(top, axis=-1, keepdims=True)
        value_copy.wait()
        mass = None
        mixed = None
        for n, j in enumerate(range(0, width, CHUNK)):
            w = jnp.exp2(scores[n] - peak)
            mass = w if mass is None else mass + w
            part = jnp.dot(
                w.astype(jnp.bfloat16), value_buf[r, j : j + CHUNK],
                preferred_element_type=jnp.float32,
            )
            mixed = part if mixed is None else mixed + part
        total = jnp.sum(mass, axis=-1, keepdims=True)
        mixed = mixed / total
        level = jnp.broadcast_to(peak + jnp.log2(total), (heads, head_dim))
        for i in range(slabs):
            state_out[r, i, 0, :own] = mixed[i * own : (i + 1) * own]
            state_out[r, i, 1, :own] = level[i * own : (i + 1) * own]
        for d in range(1, slabs):
            peer = lax.rem(ctx + d, slabs)
            pltpu.make_async_remote_copy(
                src_ref=state_out.at[r, peer], dst_ref=state_in.at[r, d - 1],
                send_sem=state_send.at[r], recv_sem=state_recv.at[r],
                device_id=(peer, section), device_id_type=MESH,
            ).start()

    def combine(r):
        wait_bytes(state_in.at[r], state_recv.at[r])
        parts = [state_out[r, ctx, 0, :own]] + [state_in[r, d, 0, :own] for d in range(slabs - 1)]
        levels = [state_out[r, ctx, 1, :own]] + [state_in[r, d, 1, :own] for d in range(slabs - 1)]
        top = functools.reduce(jnp.maximum, levels)
        shares = [jnp.exp2(level - top) for level in levels]
        mixed = sum(p * w for p, w in zip(parts, shares)) / sum(shares)

        @pl.when(has_next)
        def _():
            hand_on[r, :own] = residual[r, ctx, :own] + mixed
            for i in range(slabs):
                pltpu.make_async_remote_copy(
                    src_ref=hand_on.at[r], dst_ref=residual.at[r, ctx],
                    send_sem=hand_send.at[r], recv_sem=hand_recv.at[r],
                    device_id=(i, after), device_id_type=MESH,
                ).start()

        result[r, :own] = mixed

    def attend_turn(r, _):
        attend(r)
        return 0

    def combine_turn(r, _):
        combine(r)
        return 0

    lax.fori_loop(0, requests, attend_turn, 0)
    lax.fori_loop(0, requests, combine_turn, 0)

    for r in range(requests):
        for h in range(own):
            out[r : r + 1, h * head_dim : (h + 1) * head_dim] = result[r, h : h + 1, :]

    wait_bytes(query_all.at[arrivals, firsts], query_send.at[0])
    wait_bytes(query_all.at[arrivals, others], query_send.at[1])
    for r in range(requests):
        wait_bytes(state_in.at[r], state_send.at[r])

    @pl.when(has_next)
    def _():
        for r in range(requests):
            wait_bytes(residual.at[r], hand_send.at[r])


def body(query_in, keys, values, lengths):
    sections = lax.axis_size("section")
    slabs = lax.axis_size("ctx")
    _, requests, span, kv_heads, head_dim = keys.shape
    own = query_in.shape[2] // head_dim
    rows = -(-own // 8) * 8
    width = span * kv_heads
    dims = (slabs, sections, requests, own, kv_heads, span, head_dim, rows)
    flat_keys = keys.reshape(requests, width, head_dim)
    flat_values = values.reshape(requests, width, head_dim)
    dma = pltpu.SemaphoreType.DMA
    f32 = jnp.float32
    result = pl.pallas_call(
        functools.partial(kernel, dims),
        out_shape=jax.ShapeDtypeStruct((requests, own * head_dim), f32),
        in_specs=[
            pl.BlockSpec(memory_space=pltpu.HBM),
            pl.BlockSpec(memory_space=pltpu.HBM),
            pl.BlockSpec(memory_space=pltpu.HBM),
            pl.BlockSpec(memory_space=pltpu.HBM),
        ],
        out_specs=pl.BlockSpec(memory_space=pltpu.VMEM),
        scratch_shapes=[
            pltpu.SMEM((requests,), jnp.int32),
            pltpu.VMEM((requests, own * head_dim), jnp.bfloat16),
            pltpu.VMEM((requests, width, head_dim), jnp.bfloat16),
            pltpu.VMEM((requests, width, head_dim), jnp.bfloat16),
            pltpu.VMEM((requests, kv_heads, 8, width), f32),
            pltpu.VMEM((slabs, requests, rows, head_dim), f32),
            pltpu.VMEM((requests, slabs, rows, head_dim), f32),
            pltpu.VMEM((requests, slabs, 2, rows, head_dim), f32),
            pltpu.VMEM((requests, slabs - 1, 2, rows, head_dim), f32),
            pltpu.VMEM((requests, rows, head_dim), f32),
            pltpu.VMEM((requests, rows, head_dim), f32),
            dma((requests,)),
            dma((requests,)),
            dma((2,)),
            dma((2,)),
            dma((requests,)),
            dma((requests,)),
            dma((requests,)),
            dma((requests,)),
            dma((2,)),
        ],
        compiler_params=pltpu.CompilerParams(
            collective_id=0, has_side_effects=True, vmem_limit_bytes=60 * 1024 * 1024
        ),
        name="layered_decode",
    )(lengths[:, 0], query_in[0], flat_keys, flat_values)
    return result.astype(jnp.bfloat16)[None]


def solution(mesh):
    return jax.shard_map(
        body,
        mesh=mesh,
        in_specs=(
            P("section", None, "ctx"),
            P("section", None, "ctx", None, None),
            P("section", None, "ctx", None, None),
            P(None, "ctx"),
        ),
        out_specs=P("section", None, "ctx"),
        check_vma=False,
    )
```
